32 devices in a mesh: dp: 8 (over z, x), ctx: 4 (over y, core).
Axes of the slice: x: 2, y: 2, z: 4, core: 2. Of those that a mesh axis runs over, the one named last changes fastest.
Arguments:
- hidden: bfloat16 [8, 1024, 4096], P('dp', 'ctx'), may hold values from -6 to 6
- segments: int32 [8, 1024], P('dp', 'ctx'), may hold values from 0 to 7, as said below
- gain: float32 [4096], replicated, may hold values from 0.25 to 1.75
- inv_temp: float32 [], replicated, may hold values from 20 to 50
- positives: int32 [64], P(('dp', 'ctx')), may hold values from 0 to 63, as said below
Outputs:
- grad_hidden: bfloat16 [8, 1024, 4096], P('dp', 'ctx')
- grad_gain: float32 [4096], replicated
- loss: float32 [], replicated
The draws below stay inside these ranges and needn't reach their ends.
Inputs may be any that keep to these rules, and one draw needn't show every extreme that they name: `segments`: in each sequence the document numbers never fall along positions and every document has one position or more; document 0 covers more than half of the sequence's positions. `positives`: no document is its own positive.
All inputs are finite; a program needn't handle non-finite values.
Results may differ from the reference program's by a relative error of at most 0.0053.
Values may be sent and summed in bfloat16 or wider, within the bound.
No kernel may reach another device: no remote copies, remote signals or barrier semaphores. Data moves between devices by JAX's collectives and lax.ppermute only.
A program may use at most 64 MiB of HBM per device.

```python
import jax
import jax.numpy as jnp
from jax import lax

D = 4096
TOKENS_PER_SHARD = 256
SEQ = 1024
DOCS_SEQ = 8
ALL_DOCS = 64
N_DP = 8


def one_sequence(key):
    first_len = SEQ // 2 + 1 + jax.random.randint(jax.random.fold_in(key, 1), (), 0, TOKENS_PER_SHARD).astype(jnp.int32)
    rest = SEQ - first_len
    spots = jnp.arange(SEQ, dtype=jnp.int32)
    scores = jax.random.randint(jax.random.fold_in(key, 2), (SEQ,), 0, SEQ).astype(jnp.int32) * SEQ + spots
    valid = jnp.logical_and(spots >= 1, spots <= rest - 1)
    scores = jnp.where(valid, scores, -1)
    picked = lax.top_k(scores, DOCS_SEQ - 2)[1].astype(jnp.int32)
    offset = spots - first_len
    after_first = (spots >= first_len).astype(jnp.int32)
    crossed = jnp.sum((offset[:, None] >= picked[None, :]).astype(jnp.int32), axis=1).astype(jnp.int32)
    return (after_first + after_first * crossed).astype(jnp.int32)


def draw_segments(key, part):
    keys = jax.random.split(jax.random.fold_in(key, 11), N_DP)
    return jax.vmap(one_sequence)(keys).astype(jnp.int32)


def draw_positives(key, part):
    order = jax.random.permutation(jax.random.fold_in(key, 7), ALL_DOCS).astype(jnp.int32)
    series = jnp.arange(ALL_DOCS, dtype=jnp.int32)
    return jnp.where(order == series, (series + 1) % ALL_DOCS, order).astype(jnp.int32)


def steps_of(stream_key, shape, cuts, smallest, largest):
    def one(axis_at, parts):
        heights = jax.random.uniform(jax.random.fold_in(jax.random.fold_in(stream_key, 6), axis_at), (parts,), jnp.float32, smallest / len(cuts), largest / len(cuts))
        return jnp.repeat(jnp.exp(heights), shape[axis_at] // parts).reshape((-1,) + (1,) * (len(shape) - axis_at - 1))

    level = one(*cuts[0])
    for cut in cuts[1:]:
        level = level * one(*cut)
    return level


def normal_values(own_key, dims, width, bound, shards=(), kind=jnp.bfloat16):
    drawn = jax.random.normal(own_key, dims, jnp.float32) * width
    if len(shards) > 0:
        drawn = steps_of(own_key, dims, shards, -0.22, 0.18) * drawn
    return jnp.clip(drawn, min=-bound, max=bound).astype(kind)


def setup_inputs(seed: int = 0) -> dict:
    key_of = jax.random.split(jax.random.key(seed), 6)
    return {
        "hidden": normal_values(key_of[0], (N_DP, SEQ, D), 1.0, 6.0, ((0, 8), (1, 4))),
        "segments": draw_segments(jax.random.fold_in(key_of[5], 71), 0),
        "gain": jnp.clip(1.0 + 0.15 * jax.random.normal(key_of[2], (D,), jnp.float32), 0.25, 1.75),
        "inv_temp": jnp.clip(jax.random.uniform(key_of[3], (), jnp.float32, 20.0, 50.0), 20.0, 50.0),
        "positives": draw_positives(jax.random.fold_in(key_of[5], 71), 0),
    }


def reference(hidden, segments, gain, inv_temp, positives):
    states = hidden.astype(jnp.float32)
    scale_t = lax.rsqrt(lax.optimization_barrier(jnp.mean(states * states, axis=-1, keepdims=True)) + 1e-06)
    normalized_rows = states * scale_t * gain
    document_indicator = (segments[:, :, None] == jnp.arange(DOCS_SEQ, dtype=jnp.int32)[None, None, :]).astype(jnp.float32)
    pooled_totals = jnp.einsum('eux,euj->exj', document_indicator, normalized_rows, precision=lax.Precision.HIGHEST)
    counts = lax.optimization_barrier(jnp.sum(document_indicator, axis=1))
    pooled = (pooled_totals / counts[:, :, None]).reshape(ALL_DOCS, D)
    rnorm = lax.rsqrt(lax.optimization_barrier(jnp.sum(pooled * pooled, axis=-1, keepdims=True)) + 1e-06)
    emb_f = pooled * rnorm
    emb = emb_f.astype(jnp.bfloat16)
    logits = jnp.dot(emb, emb.T, preferred_element_type=jnp.float32) * inv_temp
    rows = jnp.arange(ALL_DOCS, dtype=jnp.int32)
    self_mask = rows[:, None] == rows[None, :]
    pos_mask = (rows[None, :] == positives[:, None]).astype(jnp.float32)
    logits = jnp.where(self_mask, -1e+30, logits)
    top = lax.optimization_barrier(jnp.max(logits, axis=1, keepdims=True))
    expo = jnp.exp(logits - top)
    total = lax.optimization_barrier(jnp.sum(expo, axis=1, keepdims=True))
    lse = top[:, 0] + jnp.log(total[:, 0])
    pos_logit = lax.optimization_barrier(jnp.sum(pos_mask * logits, axis=1))
    loss = jnp.sum(lse - pos_logit) / ALL_DOCS
    gmat = ((expo / total - pos_mask) * (inv_temp / ALL_DOCS)).astype(jnp.bfloat16)
    demb = jnp.dot(gmat, emb, preferred_element_type=jnp.float32) + jnp.dot(gmat.T, emb, preferred_element_type=jnp.float32)
    dpool = rnorm * (demb - emb_f * lax.optimization_barrier(jnp.sum(emb_f * demb, axis=-1, keepdims=True)))
    sum_gradient = dpool.reshape(N_DP, DOCS_SEQ, D) / counts[:, :, None]
    normalized_gradient = jnp.einsum('gfa,gao->gfo', document_indicator, sum_gradient, precision=lax.Precision.HIGHEST)
    grad_gain = lax.optimization_barrier(jnp.sum(normalized_gradient * states * scale_t, axis=(0, 1)))
    grad_out = normalized_gradient * gain
    inner = lax.optimization_barrier(jnp.mean(grad_out * states, axis=-1, keepdims=True))
    grad_hidden = (scale_t * grad_out - states * scale_t ** 3 * inner).astype(jnp.bfloat16)
    return (grad_hidden, grad_gain, loss)
```

```python
import functools

import jax
import jax.numpy as jnp
from jax import lax
from jax.experimental import pallas as pl
from jax.experimental.pallas import tpu as pltpu
from jax.sharding import PartitionSpec as P

EPS = 1e-06
EXTRA = 128
BASE = 16
POOL_ROWS = 64
OUT_ROWS = 64
LANES = 256
BOTH = ("dp", "ctx")
VMEM_LIMIT = 32 * 1024 * 1024
F32, BF16 = jnp.float32, jnp.bfloat16


def _pieces(size, want):
    return want if size % want == 0 else size


def _spare_rows(docs):
    return -(-3 * docs // 16) * 16


def pool_kernel(docs, positives_ref, place_ref, segments_ref, gain_ref, hidden_ref, part_ref, weights_ref, square_ref, held, acc, sems):
    tokens, width = held.shape
    rows = _pieces(tokens, POOL_ROWS)
    copies = []
    for at in range(0, tokens, rows):
        copy = pltpu.make_async_copy(hidden_ref.at[0, pl.ds(at, rows)], held.at[pl.ds(at, rows)], sems.at[at // rows])
        copy.start()
        copies.append(copy)
    segments = segments_ref[...]
    slot = lax.broadcasted_iota(jnp.int32, (128, tokens), 0)
    member_t = jnp.where((slot < 3 * docs) & (slot % docs == segments), 1.0, 0.0)
    member = jnp.transpose(member_t)
    lane = lax.broadcasted_iota(jnp.int32, (rows, 128), 1)
    for step, copy in enumerate(copies):
        at = step * rows
        copy.wait()
        states = held[at : at + rows, :].astype(F32)
        mean = jnp.sum(states * states, axis=1, keepdims=True) / width
        scale = lax.rsqrt(mean + EPS)
        weight = member[at : at + rows, :] * scale
        high = weight.astype(BF16).astype(F32)
        weight = jnp.where(lane < 2 * docs, high, weight - high)
        weights_ref[at : at + rows, :] = weight.astype(BF16)
        square_ref[at : at + rows, :] = jnp.broadcast_to(scale * scale / width, (rows, 128))
        spread = jnp.transpose(weight)[docs : 3 * docs, :].astype(BF16)
        part = lax.dot_general(spread, held[at : at + rows, :], (((1,), (0,)), ((), ())), preferred_element_type=F32)
        if step == 0:
            acc[...] = part
        else:
            acc[...] += part
    part_ref[:, :width] = (acc[:docs, :] + acc[docs:, :]) * gain_ref[...]
    count = jnp.sum(member_t[:docs, :], axis=1, keepdims=True).astype(jnp.int32)
    row = lax.broadcasted_iota(jnp.int32, (docs, EXTRA), 0)
    lane = lax.broadcasted_iota(jnp.int32, (docs, EXTRA), 1)
    own = positives_ref.shape[0]
    positive = jnp.zeros((docs, EXTRA), jnp.int32)
    for i in range(own):
        positive = jnp.where(row == place_ref[0] * own + i, positives_ref[i], positive)
    digits = jnp.where(lane == 0, count // BASE, 0)
    digits = jnp.where(lane == 1, count % BASE, digits)
    digits = jnp.where(lane == 2, positive // BASE, digits)
    digits = jnp.where(lane == 3, positive % BASE, digits)
    part_ref[:, width:] = digits.astype(F32)


def loss_kernel(docs, n_blocks, temp_ref, place_ref, *refs):
    blocks = refs[:n_blocks]
    gain_ref, weights_ref, square_ref, hidden_ref, grad_hidden_ref, grad_gain_ref, loss_ref, emb, spare, own_rows, held, out, sems = refs[n_blocks:]
    tokens, width = held.shape
    n = emb.shape[0]
    group = blocks[0].shape[0]
    load = pltpu.make_async_copy(hidden_ref.at[0], held, sems.at[0])
    load.start()
    for i, block in enumerate(blocks):
        emb[pl.ds(pl.multiple_of(place_ref[1 + i] * group, group), group), :] = block[...]
    inv_temp = temp_ref[0]
    gram = lax.dot_general(emb[:, :width], emb[:, :width], (((1,), (1,)), ((), ())), preferred_element_type=F32)
    digits = emb[:, width:].astype(F32)
    digits_t = jnp.transpose(digits)
    count_c = digits[:, 0:1] * BASE + digits[:, 1:2]
    count_r = digits_t[0:1, :] * BASE + digits_t[1:2, :]
    positive = (digits[:, 2:3] * BASE + digits[:, 3:4]).astype(jnp.int32)
    row = lax.broadcasted_iota(jnp.int32, (n, n), 0)
    column = lax.broadcasted_iota(jnp.int32, (n, n), 1)
    same = row == column
    squares = jnp.where(same, gram, 0.0)
    norm_c = lax.rsqrt(jnp.sum(squares, axis=1, keepdims=True) + EPS * count_c * count_c)
    norm_r = lax.rsqrt(jnp.sum(squares, axis=0, keepdims=True) + EPS * count_r * count_r)
    cosine = gram * norm_c * norm_r
    logits = jnp.where(same, -1e30, cosine * inv_temp)
    top = jnp.max(logits, axis=1, keepdims=True)
    expo = jnp.exp(logits - top)
    total = jnp.sum(expo, axis=1, keepdims=True)
    pos_mask = jnp.where(column == positive, 1.0, 0.0)
    terms = top + jnp.log(total) - jnp.sum(pos_mask * logits, axis=1, keepdims=True)
    loss_ref[...] = jnp.sum(terms, axis=0, keepdims=True) / n
    gmat = ((expo / total - pos_mask) * (inv_temp / n)).astype(BF16).astype(F32)
    both = gmat + jnp.transpose(gmat)
    along = jnp.sum(both * cosine, axis=1, keepdims=True)
    mix = norm_c * (both * norm_r - jnp.where(same, along * norm_r, 0.0))
    own_rows[...] = mix
    own = own_rows[pl.ds(pl.multiple_of(place_ref[0] * docs, docs), docs), :]
    mix_high, own_high = mix.astype(BF16), own.astype(BF16)
    mix_low, own_low = (mix - mix_high.astype(F32)).astype(BF16), (own - own_high.astype(F32)).astype(BF16)
    stack = jnp.concatenate([mix_high.astype(F32), mix_low.astype(F32), own_high.astype(F32), own_low.astype(F32)], axis=0).astype(BF16)
    load.wait()
    lanes = _pieces(width, LANES)
    spare_rows = spare.shape[0]
    inner = jnp.zeros((tokens, spare_rows), F32)
    for at in range(0, width, lanes):
        sums = emb[:, at : at + lanes]
        gain = gain_ref[:, at : at + lanes]
        grads = jnp.dot(stack, sums, preferred_element_type=F32)
        dsum = grads[:n, :] + grads[n : 2 * n, :]
        grad_gain_ref[:, at : at + lanes] = jnp.sum(dsum * sums.astype(F32), axis=0, keepdims=True) / gain
        mine = (grads[2 * n : 2 * n + docs, :] + grads[2 * n + docs :, :]) * gain
        high = mine.astype(BF16).astype(F32)
        parts = [high, mine - high, high]
        if spare_rows > 3 * docs:
            parts.append(jnp.zeros((spare_rows - 3 * docs, lanes), F32))
        part = jnp.concatenate(parts, axis=0).astype(BF16)
        spare[:, at : at + lanes] = part
        inner += lax.dot_general(held[:, at : at + lanes], part, (((1,), (1,)), ((), ())), preferred_element_type=F32)
    weights = weights_ref[:, :spare_rows]
    pull = jnp.sum(weights.astype(F32) * inner, axis=1, keepdims=True) * square_ref[:, 0:1]
    rows = _pieces(tokens, OUT_ROWS)
    copies = []
    for at in range(0, tokens, rows):
        for left in range(0, width, lanes):
            spread = jnp.dot(weights[at : at + rows, :], spare[:, left : left + lanes], preferred_element_type=F32)
            states = held[at : at + rows, left : left + lanes].astype(F32)
            out[at : at + rows, left : left + lanes] = (spread - states * pull[at : at + rows, :]).astype(BF16)
        copy = pltpu.make_async_copy(out.at[pl.ds(at, rows)], grad_hidden_ref.at[0, pl.ds(at, rows)], sems.at[1 + at // rows])
        copy.start()
        copies.append(copy)
    for copy in copies:
        copy.wait()


def _vmem():
    return pl.BlockSpec(memory_space=pltpu.VMEM)


def _smem():
    return pl.BlockSpec(memory_space=pltpu.SMEM)


def _any():
    return pl.BlockSpec(memory_space=pl.ANY)


def tree_sum(values):
    while len(values) > 1:
        values = [values[i] + values[i + 1] for i in range(0, len(values), 2)]
    return values[0]


def body(dp, ctx, hidden, segments, gain, inv_temp, positives):
    _, tokens, width = hidden.shape
    docs = positives.shape[0] * ctx
    n = docs * dp
    rows_out, rows_in = _pieces(tokens, OUT_ROWS), _pieces(tokens, POOL_ROWS)
    d, c = lax.axis_index("dp"), lax.axis_index("ctx")
    core = lax.rem(c, 2)
    gain = gain.reshape(1, width)

    def move(x, to):
        return lax.ppermute(x, BOTH, [(i * ctx + j, to(i, j)[0] * ctx + to(i, j)[1]) for i in range(dp) for j in range(ctx)])

    part, weights, square = pl.pallas_call(
        functools.partial(pool_kernel, docs),
        out_shape=(
            jax.ShapeDtypeStruct((docs, width + EXTRA), F32),
            jax.ShapeDtypeStruct((tokens, 128), BF16),
            jax.ShapeDtypeStruct((tokens, 128), F32),
        ),
        in_specs=[_smem(), _smem(), _vmem(), _vmem(), _any()],
        out_specs=(_vmem(), _vmem(), _vmem()),
        scratch_shapes=[
            pltpu.VMEM((tokens, width), BF16),
            pltpu.VMEM((2 * docs, width), F32),
            pltpu.SemaphoreType.DMA((tokens // rows_in,)),
        ],
        compiler_params=pltpu.CompilerParams(vmem_limit_bytes=VMEM_LIMIT),
        name="pool",
    )(positives, c.reshape(1), segments, gain, hidden)

    chip = (part + move(part, lambda i, j: (i, j ^ 1))).astype(BF16)
    found = {}
    for dx in range(2):
        for dy in range(ctx // 2):
            found[dx, dy] = chip if (dx, dy) == (0, 0) else move(chip, lambda i, j: (i ^ dx, j ^ (2 * dy)))
    here, there = (tree_sum([found[dx, dy].astype(F32) for dy in range(ctx // 2)]).astype(BF16) for dx in range(2))
    odd = lax.rem(d, 2) == 1
    pair = jnp.concatenate([jnp.where(odd, there, here), jnp.where(odd, here, there)], axis=0)

    groups = dp // 2
    g = d // 2
    blocks, places = [pair], [g]

    def swap(x):
        return move(x, lambda i, j: (i, j ^ 1))

    for k in range(1, groups - 1, 2):
        mine = move(pair, lambda i, j: (i ^ (2 * (k + j % 2)), j))
        blocks += [mine, swap(mine)]
        places += [g ^ (k + core), g ^ (k + 1 - core)]
    if groups > 1:
        half = move(jnp.where(core == 0, pair[:docs], pair[docs:]), lambda i, j: (i ^ (2 * (groups - 1)), j))
        other = swap(half)
        blocks.append(jnp.concatenate([jnp.where(core == 0, half, other), jnp.where(core == 0, other, half)], axis=0))
        places.append(g ^ (groups - 1))

    place = jnp.stack([d] + places).astype(jnp.int32)
    grad_hidden, grad_gain, loss = pl.pallas_call(
        functools.partial(loss_kernel, docs, len(blocks)),
        out_shape=(
            jax.ShapeDtypeStruct((1, tokens, width), BF16),
            jax.ShapeDtypeStruct((1, width), F32),
            jax.ShapeDtypeStruct((1, 1), F32),
        ),
        in_specs=[_smem(), _smem()] + [_vmem()] * (len(blocks) + 3) + [_any()],
        out_specs=(_any(), _vmem(), _vmem()),
        scratch_shapes=[
            pltpu.VMEM((n, width + EXTRA), BF16),
            pltpu.VMEM((_spare_rows(docs), width), BF16),
            pltpu.VMEM((n, n), F32),
            pltpu.VMEM((tokens, width), BF16),
            pltpu.VMEM((tokens, width), BF16),
            pltpu.SemaphoreType.DMA((1 + tokens // rows_out,)),
        ],
        compiler_params=pltpu.CompilerParams(vmem_limit_bytes=VMEM_LIMIT),
        name="loss",
    )(inv_temp.reshape(1), place, *blocks, gain, weights, square, hidden)
    return grad_hidden, grad_gain.reshape(width), loss.reshape(())


def solution(mesh):
    return jax.shard_map(
        functools.partial(body, mesh.shape["dp"], mesh.shape["ctx"]),
        mesh=mesh,
        in_specs=(P("dp", "ctx", None), P("dp", "ctx"), P(), P(), P(("dp", "ctx"))),
        out_specs=(P("dp", "ctx", None), P(), P()),
        check_vma=False,
    )
```

```python
import functools

import jax
import jax.numpy as jnp
from jax import lax
from jax.experimental import pallas as pl
from jax.experimental.pallas import tpu as pltpu
from jax.sharding import PartitionSpec as P

EPS = 1e-06
EXTRA = 128
BASE = 16
POOL_ROWS = 64
OUT_ROWS = 64
LANES = 256
BOTH = ("dp", "ctx")
VMEM_LIMIT = 32 * 1024 * 1024
F32, BF16 = jnp.float32, jnp.bfloat16


def _pieces(size, want):
    return want if size % want == 0 else size


def _spare_rows(docs):
    return -(-3 * docs // 16) * 16


def pool_kernel(docs, positives_hbm, segments_hbm, gain_hbm, hidden_ref, part_ref, weights_ref, square_ref, positives_ref, segments_ref, gain_ref, held, acc, sems, small_sems):
    tokens, width = held.shape
    rows = _pieces(tokens, POOL_ROWS)
    small = []
    for i, (source, target) in enumerate([(segments_hbm, segments_ref), (gain_hbm, gain_ref), (positives_hbm, positives_ref)]):
        small.append(pltpu.make_async_copy(source, target, small_sems.at[i]))
        small[-1].start()
    copies = []
    for at in range(0, tokens, rows):
        copy = pltpu.make_async_copy(hidden_ref.at[0, pl.ds(at, rows)], held.at[pl.ds(at, rows)], sems.at[at // rows])
        copy.start()
        copies.append(copy)
    small[0].wait()
    segments = segments_ref[...]
    slot = lax.broadcasted_iota(jnp.int32, (128, tokens), 0)
    member_t = jnp.where((slot < 3 * docs) & (slot % docs == segments), 1.0, 0.0)
    member = jnp.transpose(member_t)
    lane = lax.broadcasted_iota(jnp.int32, (rows, 128), 1)
    for step, copy in enumerate(copies):
        at = step * rows
        copy.wait()
        states = held[at : at + rows, :].astype(F32)
        mean = jnp.sum(states * states, axis=1, keepdims=True) / width
        scale = lax.rsqrt(mean + EPS)
        weight = member[at : at + rows, :] * scale
        high = weight.astype(BF16).astype(F32)
        weight = jnp.where(lane < 2 * docs, high, weight - high)
        weights_ref[at : at + rows, :] = weight.astype(BF16)
        square_ref[at : at + rows, :] = jnp.broadcast_to(scale * scale / width, (rows, 128))
        spread = jnp.transpose(weight)[docs : 3 * docs, :].astype(BF16)
        part = lax.dot_general(spread, held[at : at + rows, :], (((1,), (0,)), ((), ())), preferred_element_type=F32)
        if step == 0:
            acc[...] = part
        else:
            acc[...] += part
    small[1].wait()
    part_ref[:, :width] = (acc[:docs, :] + acc[docs:, :]) * gain_ref[...]
    count = jnp.sum(member_t[:docs, :], axis=1, keepdims=True).astype(jnp.int32)
    row = lax.broadcasted_iota(jnp.int32, (docs, EXTRA), 0)
    lane = lax.broadcasted_iota(jnp.int32, (docs, EXTRA), 1)
    own = positives_ref.shape[0]
    small[2].wait()
    first = lax.axis_index("ctx") * own
    positive = jnp.zeros((docs, EXTRA), jnp.int32)
    for i in range(own):
        positive = jnp.where(row == first + i, positives_ref[i], positive)
    digits = jnp.where(lane == 0, count // BASE, 0)
    digits = jnp.where(lane == 1, count % BASE, digits)
    digits = jnp.where(lane == 2, positive // BASE, digits)
    digits = jnp.where(lane == 3, positive % BASE, digits)
    part_ref[:, width:] = digits.astype(F32)


def loss_kernel(docs, n_blocks, temp_hbm, place_ref, *refs):
    blocks = refs[:n_blocks]
    gain_ref, weights_ref, square_ref, held, grad_hidden_ref, grad_gain_ref, loss_ref, temp_ref, emb, spare, own_rows, out, sems = refs[n_blocks:]
    tokens, width = out.shape
    n = emb.shape[0]
    group = blocks[0].shape[0]
    load = pltpu.make_async_copy(temp_hbm, temp_ref, sems.at[0])
    load.start()
    for i, block in enumerate(blocks):
        emb[pl.ds(pl.multiple_of(place_ref[1 + i] * group, group), group), :] = block[...]
    gram = lax.dot_general(emb[:, :width], emb[:, :width], (((1,), (1,)), ((), ())), preferred_element_type=F32)
    digits = emb[:, width:].astype(F32)
    digits_t = jnp.transpose(digits)
    count_c = digits[:, 0:1] * BASE + digits[:, 1:2]
    count_r = digits_t[0:1, :] * BASE + digits_t[1:2, :]
    positive = (digits[:, 2:3] * BASE + digits[:, 3:4]).astype(jnp.int32)
    row = lax.broadcasted_iota(jnp.int32, (n, n), 0)
    column = lax.broadcasted_iota(jnp.int32, (n, n), 1)
    same = row == column
    squares = jnp.where(same, gram, 0.0)
    norm_c = lax.rsqrt(jnp.sum(squares, axis=1, keepdims=True) + EPS * count_c * count_c)
    norm_r = lax.rsqrt(jnp.sum(squares, axis=0, keepdims=True) + EPS * count_r * count_r)
    cosine = gram * norm_c * norm_r
    load.wait()
    inv_temp = temp_ref[0]
    logits = jnp.where(same, -1e30, cosine * inv_temp)
    top = jnp.max(logits, axis=1, keepdims=True)
    expo = jnp.exp(logits - top)
    total = jnp.sum(expo, axis=1, keepdims=True)
    pos_mask = jnp.where(column == positive, 1.0, 0.0)
    terms = top + jnp.log(total) - jnp.sum(pos_mask * logits, axis=1, keepdims=True)
    loss_ref[...] = jnp.sum(terms, axis=0, keepdims=True) / n
    gmat = ((expo / total - pos_mask) * (inv_temp / n)).astype(BF16).astype(F32)
    both = gmat + jnp.transpose(gmat)
    along = jnp.sum(both * cosine, axis=1, keepdims=True)
    mix = norm_c * (both * norm_r - jnp.where(same, along * norm_r, 0.0))
    own_rows[...] = mix
    own = own_rows[pl.ds(pl.multiple_of(place_ref[0] * docs, docs), docs), :]
    mix_high, own_high = mix.astype(BF16), own.astype(BF16)
    mix_low, own_low = (mix - mix_high.astype(F32)).astype(BF16), (own - own_high.astype(F32)).astype(BF16)
    stack = jnp.concatenate([mix_high.astype(F32), mix_low.astype(F32), own_high.astype(F32), own_low.astype(F32)], axis=0).astype(BF16)
    lanes = _pieces(width, LANES)
    spare_rows = spare.shape[0]
    inner = jnp.zeros((tokens, spare_rows), F32)
    for at in range(0, width, lanes):
        sums = emb[:, at : at + lanes]
        gain = gain_ref[:, at : at + lanes]
        grads = jnp.dot(stack, sums, preferred_element_type=F32)
        dsum = grads[:n, :] + grads[n : 2 * n, :]
        grad_gain_ref[:, at : at + lanes] = jnp.sum(dsum * sums.astype(F32), axis=0, keepdims=True) / gain
        mine = (grads[2 * n : 2 * n + docs, :] + grads[2 * n + docs :, :]) * gain
        high = mine.astype(BF16).astype(F32)
        parts = [high, mine - high, high]
        if spare_rows > 3 * docs:
            parts.append(jnp.zeros((spare_rows - 3 * docs, lanes), F32))
        part = jnp.concatenate(parts, axis=0).astype(BF16)
        spare[:, at : at + lanes] = part
        inner += lax.dot_general(held[0, :, at : at + lanes], part, (((1,), (1,)), ((), ())), preferred_element_type=F32)
    weights = weights_ref[:, :spare_rows]
    pull = jnp.sum(weights.astype(F32) * inner, axis=1, keepdims=True) * square_ref[:, 0:1]
    rows = _pieces(tokens, OUT_ROWS)
    copies = []
    for at in range(0, tokens, rows):
        for left in range(0, width, lanes):
            spread = jnp.dot(weights[at : at + rows, :], spare[:, left : left + lanes], preferred_element_type=F32)
            states = held[0, at : at + rows, left : left + lanes].astype(F32)
            out[at : at + rows, left : left + lanes] = (spread - states * pull[at : at + rows, :]).astype(BF16)
        copy = pltpu.make_async_copy(out.at[pl.ds(at, rows)], grad_hidden_ref.at[0, pl.ds(at, rows)], sems.at[1 + at // rows])
        copy.start()
        copies.append(copy)
    for copy in copies:
        copy.wait()


def _vmem():
    return pl.BlockSpec(memory_space=pltpu.VMEM)


def _smem():
    return pl.BlockSpec(memory_space=pltpu.SMEM)


def _hbm():
    return pl.BlockSpec(memory_space=pltpu.HBM)


def tree_sum(values):
    while len(values) > 1:
        values = [values[i] + values[i + 1] for i in range(0, len(values), 2)]
    return values[0]


def body(dp, ctx, hidden, segments, gain, inv_temp, positives):
    _, tokens, width = hidden.shape
    docs = positives.shape[0] * ctx
    n = docs * dp
    rows_out, rows_in = _pieces(tokens, OUT_ROWS), _pieces(tokens, POOL_ROWS)
    d, c = lax.axis_index("dp"), lax.axis_index("ctx")
    core = lax.rem(c, 2)
    gain = gain.reshape(1, width)

    def move(x, to):
        return lax.ppermute(x, BOTH, [(i * ctx + j, to(i, j)[0] * ctx + to(i, j)[1]) for i in range(dp) for j in range(ctx)])

    part, weights, square = pl.pallas_call(
        functools.partial(pool_kernel, docs),
        out_shape=(
            jax.ShapeDtypeStruct((docs, width + EXTRA), F32),
            jax.ShapeDtypeStruct((tokens, 128), BF16),
            jax.ShapeDtypeStruct((tokens, 128), F32),
        ),
        in_specs=[_hbm()] * 4,
        out_specs=(_vmem(), _vmem(), _vmem()),
        scratch_shapes=[
            pltpu.SMEM(positives.shape, jnp.int32),
            pltpu.VMEM((1, tokens), jnp.int32),
            pltpu.VMEM((1, width), F32),
            pltpu.VMEM((tokens, width), BF16),
            pltpu.VMEM((2 * docs, width), F32),
            pltpu.SemaphoreType.DMA((tokens // rows_in,)),
            pltpu.SemaphoreType.DMA((3,)),
        ],
        compiler_params=pltpu.CompilerParams(vmem_limit_bytes=VMEM_LIMIT),
        name="pool",
    )(*(pltpu.with_memory_space_constraint(x, pltpu.HBM) for x in (positives, segments, gain, hidden)))

    chip = (part + move(part, lambda i, j: (i, j ^ 1))).astype(BF16)
    found = {}
    for dx in range(2):
        for dy in range(ctx // 2):
            found[dx, dy] = chip if (dx, dy) == (0, 0) else move(chip, lambda i, j: (i ^ dx, j ^ (2 * dy)))
    here, there = (tree_sum([found[dx, dy].astype(F32) for dy in range(ctx // 2)]).astype(BF16) for dx in range(2))
    odd = lax.rem(d, 2) == 1
    pair = jnp.concatenate([jnp.where(odd, there, here), jnp.where(odd, here, there)], axis=0)

    groups = dp // 2
    g = d // 2
    blocks, places = [pair], [g]

    def swap(x):
        return move(x, lambda i, j: (i, j ^ 1))

    for k in range(1, groups - 1, 2):
        mine = move(pair, lambda i, j: (i ^ (2 * (k + j % 2)), j))
        blocks += [mine, swap(mine)]
        places += [g ^ (k + core), g ^ (k + 1 - core)]
    if groups > 1:
        half = move(jnp.where(core == 0, pair[:docs], pair[docs:]), lambda i, j: (i ^ (2 * (groups - 1)), j))
        other = swap(half)
        blocks.append(jnp.concatenate([jnp.where(core == 0, half, other), jnp.where(core == 0, other, half)], axis=0))
        places.append(g ^ (groups - 1))

    place = jnp.stack([d] + places).astype(jnp.int32)
    grad_hidden, grad_gain, loss = pl.pallas_call(
        functools.partial(loss_kernel, docs, len(blocks)),
        out_shape=(
            jax.ShapeDtypeStruct((1, tokens, width), BF16),
            jax.ShapeDtypeStruct((1, width), F32),
            jax.ShapeDtypeStruct((1, 1), F32),
        ),
        in_specs=[_hbm(), _smem()] + [_vmem()] * (len(blocks) + 4),
        out_specs=(_hbm(), _vmem(), _vmem()),
        scratch_shapes=[
            pltpu.SMEM((1,), F32),
            pltpu.VMEM((n, width + EXTRA), BF16),
            pltpu.VMEM((_spare_rows(docs), width), BF16),
            pltpu.VMEM((n, n), F32),
            pltpu.VMEM((tokens, width), BF16),
            pltpu.SemaphoreType.DMA((1 + tokens // rows_out,)),
        ],
        compiler_params=pltpu.CompilerParams(vmem_limit_bytes=VMEM_LIMIT),
        name="loss",
    )(inv_temp.reshape(1), place, *blocks, gain, weights, square, hidden)
    return grad_hidden, grad_gain.reshape(width), loss.reshape(())


def solution(mesh):
    return jax.shard_map(
        functools.partial(body, mesh.shape["dp"], mesh.shape["ctx"]),
        mesh=mesh,
        in_specs=(P("dp", "ctx", None), P("dp", "ctx"), P(), P(), P(("dp", "ctx"))),
        out_specs=(P("dp", "ctx", None), P(), P()),
        check_vma=False,
    )
```

```python
import functools

import jax
import jax.numpy as jnp
from jax import lax
from jax.experimental import pallas as pl
from jax.experimental.pallas import tpu as pltpu
from jax.sharding import PartitionSpec as P

EPS = 1e-06
EXTRA = 128
BASE = 16
POOL_ROWS = 64
OUT_LANES = 1024
LANES = 256
BOTH = ("dp", "ctx")
VMEM_LIMIT = 32 * 1024 * 1024
F32, BF16 = jnp.float32, jnp.bfloat16


def _pieces(size, want):
    return want if size % want == 0 else size


def pool_kernel(docs, n, *refs):
    hidden_ref, *inputs, part_ref, onehot_ref, side_ref, held = refs[:8]
    segments_ref, gain_ref, positives_ref, acc, sems, small_sems = refs[8:]
    tokens, width = held.shape
    rows = _pieces(tokens, POOL_ROWS)
    small = []
    for i, (source, target) in enumerate(zip(inputs, (segments_ref, gain_ref, positives_ref), strict=True)):
        small.append(pltpu.make_async_copy(source, target, small_sems.at[i]))
        small[-1].start()
    copies = []
    for at in range(0, tokens, rows):
        copy = pltpu.make_async_copy(hidden_ref.at[0, pl.ds(at, rows)], held.at[pl.ds(at, rows)], sems.at[at // rows])
        copy.start()
        copies.append(copy)
    rank = lax.axis_index("dp")
    small[0].wait()
    segments = segments_ref[...]
    member = jnp.where(lax.broadcasted_iota(jnp.int32, (docs, tokens), 0) == segments, 1.0, 0.0)
    count = jnp.sum(member, axis=1, keepdims=True).astype(jnp.int32)
    document = jnp.transpose(jnp.broadcast_to(segments.astype(F32), (128, tokens)))[:, 0:1].astype(jnp.int32) + rank * docs
    lane = lax.broadcasted_iota(jnp.int32, onehot_ref.shape, 1)
    onehot_ref[...] = jnp.where(lax.rem(lane, n) == document, 1.0, 0.0).astype(BF16)
    lane = lax.broadcasted_iota(jnp.int32, (rows, 128), 1)
    for step, copy in enumerate(copies):
        at = step * rows
        copy.wait()
        states = held[at : at + rows, :].astype(F32)
        mean = jnp.sum(states * states, axis=1, keepdims=True) / width
        scale = lax.rsqrt(mean + EPS)
        side_ref[at : at + rows, :] = jnp.where(lane == 0, scale, scale * scale / width)
        scale_t = jnp.transpose(jnp.broadcast_to(scale, (rows, 128)))[:docs, :]
        weight = member[:, at : at + rows] * scale_t
        high = weight.astype(BF16).astype(F32)
        weight = jnp.concatenate([high, weight - high], axis=0).astype(BF16)
        part = jnp.dot(weight, held[at : at + rows, :], preferred_element_type=F32)
        if step == 0:
            acc[...] = part
        else:
            acc[...] += part
    small[1].wait()
    part_ref[:, :width] = (acc[:docs, :] + acc[docs:, :]) * gain_ref[...]
    small[2].wait()
    row = lax.broadcasted_iota(jnp.int32, (docs, EXTRA), 0)
    lane = lax.broadcasted_iota(jnp.int32, (docs, EXTRA), 1)
    own = positives_ref.shape[0]
    first = lax.axis_index("ctx") * own
    positive = jnp.zeros((docs, EXTRA), jnp.int32)
    for i in range(own):
        positive = jnp.where(row == first + i, positives_ref[i], positive)
    digits = jnp.where(lane == 0, count // BASE, 0)
    digits = jnp.where(lane == 1, count % BASE, digits)
    digits = jnp.where(lane == 2, positive // BASE, digits)
    digits = jnp.where(lane == 3, positive % BASE, digits)
    part_ref[:, width:] = digits.astype(F32)


def block_groups(n_blocks, groups):
    core = lax.rem(lax.axis_index("ctx"), 2)
    own = lax.div(lax.axis_index("dp"), 2)
    places = [own]
    for k in range(1, groups - 1, 2):
        places += [own ^ (k + core), own ^ (k + 1 - core)]
    if groups > 1:
        places.append(own ^ (groups - 1))
    return places[:n_blocks]


def _high_low(x):
    high = x.astype(BF16).astype(F32)
    return high, x - high


def loss_kernel(n_blocks, *refs):
    blocks = refs[:n_blocks]
    temp_ref, gain_ref, onehot_ref, side_ref, held, grad_hidden_hbm, grad_gain_hbm, loss_hbm = refs[n_blocks : n_blocks + 8]
    emb, scaled, out, grad_gain, loss, sems = refs[n_blocks + 8 :]
    tokens, width = out.shape
    n = emb.shape[0]
    lanes = _pieces(width, LANES)
    group = blocks[0].shape[0]
    for place, block in zip(block_groups(n_blocks, n // group), blocks, strict=True):
        emb[pl.ds(pl.multiple_of(place * group, group), group), :] = block[...]
    gram = lax.dot_general(emb[:, :width], emb[:, :width], (((1,), (1,)), ((), ())), preferred_element_type=F32)
    digits = emb[:, width:].astype(F32)
    digits_t = jnp.transpose(digits)
    count_c = digits[:, 0:1] * BASE + digits[:, 1:2]
    count_r = digits_t[0:1, :] * BASE + digits_t[1:2, :]
    positive_c = (digits[:, 2:3] * BASE + digits[:, 3:4]).astype(jnp.int32)
    positive_r = (digits_t[2:3, :] * BASE + digits_t[3:4, :]).astype(jnp.int32)
    row = lax.broadcasted_iota(jnp.int32, (n, n), 0)
    column = lax.broadcasted_iota(jnp.int32, (n, n), 1)
    same = row == column

    products = jnp.zeros((tokens, n), F32)
    for at in range(0, width, lanes):
        high, low = _high_low(emb[:, at : at + lanes].astype(F32) * gain_ref[:, at : at + lanes])
        high, low = high.astype(BF16), low.astype(BF16)
        scaled[:n, at : at + lanes] = high
        scaled[n : 2 * n, at : at + lanes] = low
        scaled[2 * n :, at : at + lanes] = high
        products += lax.dot_general(held[:, at : at + lanes], high, (((1,), (1,)), ((), ())), preferred_element_type=F32)

    squares = jnp.where(same, gram, 0.0)
    norm_c = lax.rsqrt(jnp.sum(squares, axis=1, keepdims=True) + EPS * count_c * count_c)
    norm_r = lax.rsqrt(jnp.sum(squares, axis=0, keepdims=True) + EPS * count_r * count_r)
    cosine = gram * norm_c * norm_r
    inv_temp = temp_ref[0]
    logits = jnp.where(same, -1e30, cosine * inv_temp)

    def softmax(axis):
        top = jnp.max(logits, axis=axis, keepdims=True)
        expo = jnp.exp(logits - top)
        total = jnp.sum(expo, axis=axis, keepdims=True)
        return top, expo, total

    top, expo, total = softmax(1)
    _, expo_r, total_r = softmax(0)
    pos_c = jnp.where(column == positive_c, 1.0, 0.0)
    pos_r = jnp.where(row == positive_r, 1.0, 0.0)
    terms = top + jnp.log(total) - jnp.sum(pos_c * logits, axis=1, keepdims=True)
    loss[...] = jnp.sum(terms, axis=0, keepdims=True) / n
    loss_copy = pltpu.make_async_copy(loss, loss_hbm, sems.at[0])
    loss_copy.start()
    gmat = ((expo / total - pos_c) * (inv_temp / n)).astype(BF16).astype(F32)
    gmat_t = ((expo_r / total_r - pos_r) * (inv_temp / n)).astype(BF16).astype(F32)
    both = gmat + gmat_t
    along = jnp.sum(both * cosine, axis=1, keepdims=True)
    mix_high, mix_low = _high_low(norm_c * norm_r * (both - jnp.where(same, along, 0.0)))
    mix = jnp.concatenate([mix_high, mix_low], axis=0).astype(BF16)

    wide = jnp.dot(onehot_ref[...], jnp.concatenate([mix] * 3, axis=1), preferred_element_type=F32) * side_ref[:, 0:1]
    pull = jnp.sum(wide[:, :n] * products, axis=1, keepdims=True) * side_ref[:, 1:2]
    high, low = _high_low(wide)
    wide = jnp.where(lax.broadcasted_iota(jnp.int32, wide.shape, 1) < 2 * n, high, low).astype(BF16)
    copies = [loss_copy]
    chunk = _pieces(width, OUT_LANES)
    for left in range(0, width, chunk):
        for at in range(left, left + chunk, lanes):
            spread = jnp.dot(wide, scaled[:, at : at + lanes], preferred_element_type=F32)
            out[:, at : at + lanes] = (spread - held[:, at : at + lanes].astype(F32) * pull).astype(BF16)
            sums = emb[:, at : at + lanes]
            grads = jnp.dot(mix, sums, preferred_element_type=F32)
            grads = jnp.sum((grads[:n, :] + grads[n:, :]) * sums.astype(F32), axis=0, keepdims=True)
            grad_gain[:, at : at + lanes] = grads / gain_ref[:, at : at + lanes]
        copy = pltpu.make_async_copy(
            out.at[:, pl.ds(left, chunk)], grad_hidden_hbm.at[0, :, pl.ds(left, chunk)], sems.at[2 + left // chunk]
        )
        copy.start()
        copies.append(copy)
    copies.append(pltpu.make_async_copy(grad_gain, grad_gain_hbm, sems.at[1]))
    copies[-1].start()
    for copy in copies:
        copy.wait()


def _vmem():
    return pl.BlockSpec(memory_space=pltpu.VMEM)


def _hbm():
    return pl.BlockSpec(memory_space=pltpu.HBM)


def tree_sum(values):
    while len(values) > 1:
        values = [values[i] + values[i + 1] for i in range(0, len(values), 2)]
    return values[0]


def body(dp, ctx, hidden, segments, gain, inv_temp, positives):
    _, tokens, width = hidden.shape
    docs = positives.shape[0] * ctx
    n = docs * dp
    rows = _pieces(tokens, POOL_ROWS)
    d, c = lax.axis_index("dp"), lax.axis_index("ctx")
    core = lax.rem(c, 2)
    gain = gain.reshape(1, width)

    def move(x, to):
        return lax.ppermute(x, BOTH, [(i * ctx + j, to(i, j)[0] * ctx + to(i, j)[1]) for i in range(dp) for j in range(ctx)])

    part, onehot, side, held = pl.pallas_call(
        functools.partial(pool_kernel, docs, n),
        out_shape=(
            jax.ShapeDtypeStruct((docs, width + EXTRA), F32),
            jax.ShapeDtypeStruct((tokens, 2 * n), BF16),
            jax.ShapeDtypeStruct((tokens, 128), F32),
            jax.ShapeDtypeStruct((tokens, width), BF16),
        ),
        in_specs=[_hbm()] * 4,
        out_specs=[_vmem()] * 4,
        scratch_shapes=[
            pltpu.VMEM((1, tokens), jnp.int32),
            pltpu.VMEM((1, width), F32),
            pltpu.SMEM(positives.shape, jnp.int32),
            pltpu.VMEM((2 * docs, width), F32),
            pltpu.SemaphoreType.DMA((tokens // rows,)),
            pltpu.SemaphoreType.DMA((3,)),
        ],
        compiler_params=pltpu.CompilerParams(vmem_limit_bytes=VMEM_LIMIT),
        name="pool",
    )(*(pltpu.with_memory_space_constraint(x, pltpu.HBM) for x in (hidden, segments, gain, positives)))

    chip = (part + move(part, lambda i, j: (i, j ^ 1))).astype(BF16)
    found = {}
    for dx in range(2):
        for dy in range(ctx // 2):
            found[dx, dy] = chip if (dx, dy) == (0, 0) else move(chip, lambda i, j: (i ^ dx, j ^ (2 * dy)))
    here, there = (tree_sum([found[dx, dy].astype(F32) for dy in range(ctx // 2)]).astype(BF16) for dx in range(2))
    odd = lax.rem(d, 2) == 1
    pair = jnp.concatenate([jnp.where(odd, there, here), jnp.where(odd, here, there)], axis=0)

    groups = dp // 2
    blocks = [pair]

    def swap(x):
        return move(x, lambda i, j: (i, j ^ 1))

    for k in range(1, groups - 1, 2):
        mine = move(pair, lambda i, j: (i ^ (2 * (k + j % 2)), j))
        blocks += [mine, swap(mine)]
    if groups > 1:
        half = move(jnp.where(core == 0, pair[:docs], pair[docs:]), lambda i, j: (i ^ (2 * (groups - 1)), j))
        other = swap(half)
        blocks.append(jnp.concatenate([jnp.where(core == 0, half, other), jnp.where(core == 0, other, half)], axis=0))

    grad_hidden, grad_gain, loss = pl.pallas_call(
        functools.partial(loss_kernel, len(blocks)),
        out_shape=(
            jax.ShapeDtypeStruct((1, tokens, width), BF16),
            jax.ShapeDtypeStruct((1, width), F32),
            jax.ShapeDtypeStruct((1, 1), F32),
        ),
        in_specs=[_vmem()] * len(blocks) + [pl.BlockSpec(memory_space=pltpu.SMEM)] + [_vmem()] * 4,
        out_specs=(_hbm(), _hbm(), _hbm()),
        scratch_shapes=[
            pltpu.VMEM((n, width + EXTRA), BF16),
            pltpu.VMEM((3 * n, width), BF16),
            pltpu.VMEM((tokens, width), BF16),
            pltpu.VMEM((1, width), F32),
            pltpu.VMEM((1, 1), F32),
            pltpu.SemaphoreType.DMA((2 + width // _pieces(width, OUT_LANES),)),
        ],
        compiler_params=pltpu.CompilerParams(vmem_limit_bytes=VMEM_LIMIT),
        name="loss",
    )(*blocks, inv_temp.reshape(1), gain, onehot, side, held)
    return grad_hidden, grad_gain.reshape(width), loss.reshape(())


def solution(mesh):
    return jax.shard_map(
        functools.partial(body, mesh.shape["dp"], mesh.shape["ctx"]),
        mesh=mesh,
        in_specs=(P("dp", "ctx", None), P("dp", "ctx"), P(), P(), P(("dp", "ctx"))),
        out_specs=(P("dp", "ctx", None), P(), P()),
        check_vma=False,
    )
```

```python
import functools

import jax
import jax.numpy as jnp
from jax import lax
from jax.experimental import pallas as pl
from jax.experimental.pallas import tpu as pltpu
from jax.sharding import PartitionSpec as P

EPS = 1e-06
EXTRA = 128
BASE = 16
POOL_ROWS = 128
OUT_LANES = 1024
LANES = 256
BOTH = ("dp", "ctx")
VMEM_LIMIT = 32 * 1024 * 1024
F32, BF16 = jnp.float32, jnp.bfloat16


def _pieces(size, want):
    return want if size % want == 0 else size


def pool_kernel(docs, n, *refs):
    hidden_ref, *inputs, part_ref, onehot_ref, side_ref, held = refs[:8]
    segments_ref, gain_ref, positives_ref, acc, sems, small_sems = refs[8:]
    tokens, width = held.shape
    rows = _pieces(tokens, POOL_ROWS)
    small = []
    for i, (source, target) in enumerate(zip(inputs, (segments_ref, gain_ref, positives_ref), strict=True)):
        small.append(pltpu.make_async_copy(source, target, small_sems.at[i]))
        small[-1].start()
    copies = []
    for at in range(0, tokens, rows):
        copy = pltpu.make_async_copy(hidden_ref.at[0, pl.ds(at, rows)], held.at[pl.ds(at, rows)], sems.at[at // rows])
        copy.start()
        copies.append(copy)
    rank = lax.axis_index("dp")
    small[0].wait()
    segments = segments_ref[...]
    member = jnp.where(lax.broadcasted_iota(jnp.int32, (docs, tokens), 0) == segments, 1.0, 0.0)
    count = jnp.sum(member, axis=1, keepdims=True).astype(jnp.int32)
    document = jnp.transpose(jnp.broadcast_to(segments.astype(F32), (128, tokens)))[:, 0:1].astype(jnp.int32) + rank * docs
    lane = lax.broadcasted_iota(jnp.int32, onehot_ref.shape, 1)
    onehot_ref[...] = jnp.where(lax.rem(lane, n) == document, 1.0, 0.0).astype(BF16)
    lane = lax.broadcasted_iota(jnp.int32, (rows, 128), 1)
    for step, copy in enumerate(copies):
        at = step * rows
        copy.wait()
        states = held[at : at + rows, :].astype(F32)
        mean = jnp.sum(states * states, axis=1, keepdims=True) / width
        scale = lax.rsqrt(mean + EPS)
        side_ref[at : at + rows, :] = jnp.where(lane == 0, scale, scale * scale / width)
        scale_t = jnp.transpose(jnp.broadcast_to(scale, (rows, 128)))[:docs, :]
        weight = member[:, at : at + rows] * scale_t
        high = weight.astype(BF16).astype(F32)
        weight = jnp.concatenate([high, weight - high], axis=0).astype(BF16)
        part = jnp.dot(weight, held[at : at + rows, :], preferred_element_type=F32)
        if step == 0:
            acc[...] = part
        else:
            acc[...] += part
    small[1].wait()
    part_ref[:, :width] = (acc[:docs, :] + acc[docs:, :]) * gain_ref[...]
    small[2].wait()
    row = lax.broadcasted_iota(jnp.int32, (docs, EXTRA), 0)
    lane = lax.broadcasted_iota(jnp.int32, (docs, EXTRA), 1)
    own = positives_ref.shape[0]
    first = lax.axis_index("ctx") * own
    positive = jnp.zeros((docs, EXTRA), jnp.int32)
    for i in range(own):
        positive = jnp.where(row == first + i, positives_ref[i], positive)
    digits = jnp.where(lane == 0, count // BASE, 0)
    digits = jnp.where(lane == 1, count % BASE, digits)
    digits = jnp.where(lane == 2, positive // BASE, digits)
    digits = jnp.where(lane == 3, positive % BASE, digits)
    part_ref[:, width:] = digits.astype(F32)


def _high_low(x):
    high = x.astype(BF16).astype(F32)
    return high, x - high


def loss_kernel(n_blocks, *refs):
    blocks = refs[:n_blocks]
    temp_ref, gain_ref, onehot_ref, side_ref, held, grad_hidden_hbm, grad_gain_hbm, loss_hbm = refs[n_blocks : n_blocks + 8]
    emb, scaled, out, grad_gain, loss, sems = refs[n_blocks + 8 :]
    tokens, width = out.shape
    n = emb.shape[0]
    lanes = _pieces(width, LANES)
    group = blocks[0].shape[0]
    own, others = lax.div(lax.axis_index("dp"), 2), n // group
    emb[pl.ds(pl.multiple_of(own * group, group), group), :] = blocks[0][...]
    for k in range(1, others):
        at = (others - 1 - k) * group
        emb[pl.ds(pl.multiple_of((own ^ k) * group, group), group), :] = blocks[1][at : at + group, :]
    gram = lax.dot_general(emb[:, :width], emb[:, :width], (((1,), (1,)), ((), ())), preferred_element_type=F32)
    digits = emb[:, width:].astype(F32)
    digits_t = jnp.transpose(digits)
    count_c = digits[:, 0:1] * BASE + digits[:, 1:2]
    count_r = digits_t[0:1, :] * BASE + digits_t[1:2, :]
    positive_c = (digits[:, 2:3] * BASE + digits[:, 3:4]).astype(jnp.int32)
    positive_r = (digits_t[2:3, :] * BASE + digits_t[3:4, :]).astype(jnp.int32)
    row = lax.broadcasted_iota(jnp.int32, (n, n), 0)
    column = lax.broadcasted_iota(jnp.int32, (n, n), 1)
    same = row == column

    products = jnp.zeros((tokens, n), F32)
    for at in range(0, width, lanes):
        high, low = _high_low(emb[:, at : at + lanes].astype(F32) * gain_ref[:, at : at + lanes])
        high, low = high.astype(BF16), low.astype(BF16)
        scaled[:n, at : at + lanes] = high
        scaled[n : 2 * n, at : at + lanes] = low
        scaled[2 * n :, at : at + lanes] = high
        products += lax.dot_general(held[:, at : at + lanes], high, (((1,), (1,)), ((), ())), preferred_element_type=F32)

    squares = jnp.where(same, gram, 0.0)
    norm_c = lax.rsqrt(jnp.sum(squares, axis=1, keepdims=True) + EPS * count_c * count_c)
    norm_r = lax.rsqrt(jnp.sum(squares, axis=0, keepdims=True) + EPS * count_r * count_r)
    cosine = gram * norm_c * norm_r
    inv_temp = temp_ref[0]
    logits = jnp.where(same, -1e30, cosine * inv_temp)

    def softmax(axis):
        top = jnp.max(logits, axis=axis, keepdims=True)
        expo = jnp.exp(logits - top)
        total = jnp.sum(expo, axis=axis, keepdims=True)
        return top, expo, total

    top, expo, total = softmax(1)
    _, expo_r, total_r = softmax(0)
    pos_c = jnp.where(column == positive_c, 1.0, 0.0)
    pos_r = jnp.where(row == positive_r, 1.0, 0.0)
    terms = top + jnp.log(total) - jnp.sum(pos_c * logits, axis=1, keepdims=True)
    loss[...] = jnp.sum(terms, axis=0, keepdims=True) / n
    loss_copy = pltpu.make_async_copy(loss, loss_hbm, sems.at[0])
    loss_copy.start()
    gmat = ((expo / total - pos_c) * (inv_temp / n)).astype(BF16).astype(F32)
    gmat_t = ((expo_r / total_r - pos_r) * (inv_temp / n)).astype(BF16).astype(F32)
    both = gmat + gmat_t
    along = jnp.sum(both * cosine, axis=1, keepdims=True)
    mix_high, mix_low = _high_low(norm_c * norm_r * (both - jnp.where(same, along, 0.0)))
    mix = jnp.concatenate([mix_high, mix_low], axis=0).astype(BF16)

    wide = jnp.dot(onehot_ref[...], jnp.concatenate([mix] * 3, axis=1), preferred_element_type=F32) * side_ref[:, 0:1]
    pull = jnp.sum(wide[:, :n] * products, axis=1, keepdims=True) * side_ref[:, 1:2]
    high, low = _high_low(wide)
    wide = jnp.where(lax.broadcasted_iota(jnp.int32, wide.shape, 1) < 2 * n, high, low).astype(BF16)
    copies = [loss_copy]
    chunk = _pieces(width, OUT_LANES)
    for left in range(0, width, chunk):
        for at in range(left, left + chunk, lanes):
            spread = jnp.dot(wide, scaled[:, at : at + lanes], preferred_element_type=F32)
            out[:, at : at + lanes] = (spread - held[:, at : at + lanes].astype(F32) * pull).astype(BF16)
            sums = emb[:, at : at + lanes]
            grads = jnp.dot(mix, sums, preferred_element_type=F32)
            grads = jnp.sum((grads[:n, :] + grads[n:, :]) * sums.astype(F32), axis=0, keepdims=True)
            grad_gain[:, at : at + lanes] = grads / gain_ref[:, at : at + lanes]
        copy = pltpu.make_async_copy(
            out.at[:, pl.ds(left, chunk)], grad_hidden_hbm.at[0, :, pl.ds(left, chunk)], sems.at[2 + left // chunk]
        )
        copy.start()
        copies.append(copy)
    copies.append(pltpu.make_async_copy(grad_gain, grad_gain_hbm, sems.at[1]))
    copies[-1].start()
    for copy in copies:
        copy.wait()


def _vmem():
    return pl.BlockSpec(memory_space=pltpu.VMEM)


def _hbm():
    return pl.BlockSpec(memory_space=pltpu.HBM)


def tree_sum(values):
    while len(values) > 1:
        values = [values[i] + values[i + 1] for i in range(0, len(values), 2)]
    return values[0]


def body(dp, ctx, hidden, segments, gain, inv_temp, positives):
    _, tokens, width = hidden.shape
    docs = positives.shape[0] * ctx
    n = docs * dp
    rows = _pieces(tokens, POOL_ROWS)
    d, c = lax.axis_index("dp"), lax.axis_index("ctx")
    core = lax.rem(c, 2)
    gain = gain.reshape(1, width)

    def move(x, to):
        return lax.ppermute(x, BOTH, [(i * ctx + j, to(i, j)[0] * ctx + to(i, j)[1]) for i in range(dp) for j in range(ctx)])

    part, onehot, side, held = pl.pallas_call(
        functools.partial(pool_kernel, docs, n),
        out_shape=(
            jax.ShapeDtypeStruct((docs, width + EXTRA), F32),
            jax.ShapeDtypeStruct((tokens, 2 * n), BF16),
            jax.ShapeDtypeStruct((tokens, 128), F32),
            jax.ShapeDtypeStruct((tokens, width), BF16),
        ),
        in_specs=[_hbm()] * 4,
        out_specs=[_vmem()] * 4,
        scratch_shapes=[
            pltpu.VMEM((1, tokens), jnp.int32),
            pltpu.VMEM((1, width), F32),
            pltpu.SMEM(positives.shape, jnp.int32),
            pltpu.VMEM((2 * docs, width), F32),
            pltpu.SemaphoreType.DMA((tokens // rows,)),
            pltpu.SemaphoreType.DMA((3,)),
        ],
        compiler_params=pltpu.CompilerParams(vmem_limit_bytes=VMEM_LIMIT),
        name="pool",
    )(*(pltpu.with_memory_space_constraint(x, pltpu.HBM) for x in (hidden, segments, gain, positives)))

    def swap(x):
        return move(x, lambda i, j: (i, j ^ 1))

    chip = (part + swap(part)).astype(BF16)
    lines = ctx // 2
    found = []
    for k in range(lines):
        own = k + 1 if k + 1 < lines else 1
        found.append(move(chip, lambda i, j: (i ^ 1, j ^ (2 * k)) if j % 2 else (i, j ^ (2 * own))))
    terms = [jnp.where(core == 0, left, right) for left, right in zip([chip] + found[:-1], found, strict=True)]
    block = tree_sum([x.astype(F32) for x in terms]).astype(BF16)

    groups = dp // 2
    even = lax.rem(core + d, 2) == 0

    def both(mine, theirs):
        pairs = jnp.stack([jnp.where(even, mine, theirs), jnp.where(even, theirs, mine)], axis=1)
        return pairs.reshape(-1, width + EXTRA)

    far = [move(block, lambda i, j: (i ^ (2 * k), j)) for k in range(groups - 1, 0, -1)]
    blocks = [both(block[None], swap(block)[None])]
    if far:
        far = jnp.stack(far)
        blocks.append(both(far, swap(far)))

    grad_hidden, grad_gain, loss = pl.pallas_call(
        functools.partial(loss_kernel, len(blocks)),
        out_shape=(
            jax.ShapeDtypeStruct((1, tokens, width), BF16),
            jax.ShapeDtypeStruct((1, width), F32),
            jax.ShapeDtypeStruct((1, 1), F32),
        ),
        in_specs=[_vmem()] * len(blocks) + [pl.BlockSpec(memory_space=pltpu.SMEM)] + [_vmem()] * 4,
        out_specs=(_hbm(), _hbm(), _hbm()),
        scratch_shapes=[
            pltpu.VMEM((n, width + EXTRA), BF16),
            pltpu.VMEM((3 * n, width), BF16),
            pltpu.VMEM((tokens, width), BF16),
            pltpu.VMEM((1, width), F32),
            pltpu.VMEM((1, 1), F32),
            pltpu.SemaphoreType.DMA((2 + width // _pieces(width, OUT_LANES),)),
        ],
        compiler_params=pltpu.CompilerParams(vmem_limit_bytes=VMEM_LIMIT),
        name="loss",
    )(*blocks, inv_temp.reshape(1), gain, onehot, side, held)
    return grad_hidden, grad_gain.reshape(width), loss.reshape(())


def solution(mesh):
    return jax.shard_map(
        functools.partial(body, mesh.shape["dp"], mesh.shape["ctx"]),
        mesh=mesh,
        in_specs=(P("dp", "ctx", None), P("dp", "ctx"), P(), P(), P(("dp", "ctx"))),
        out_specs=(P("dp", "ctx", None), P(), P()),
        check_vma=False,
    )
```

```python
import functools

import jax
import jax.numpy as jnp
from jax import lax
from jax.experimental import pallas as pl
from jax.experimental.pallas import tpu as pltpu
from jax.sharding import PartitionSpec as P

EPS = 1e-06
EXTRA = 128
BASE = 16
POOL_ROWS = 128
POOL_LANES = 1024
OUT_LANES = 512
LANES = 256
BOTH = ("dp", "ctx")
VMEM_LIMIT = 32 * 1024 * 1024
F32, BF16 = jnp.float32, jnp.bfloat16


def _pieces(size, want):
    return want if size % want == 0 else size


def _high_low(x):
    high = x.astype(BF16).astype(F32)
    return high, x - high


def pool_kernel(docs, n, *refs):
    hidden_ref, *inputs, part_ref, onehot_ref, side_ref, held = refs[:8]
    segments_ref, gain_ref, positives_ref, sems, small_sems = refs[8:]
    tokens, width = held.shape
    rows = _pieces(tokens, POOL_ROWS)
    small = []
    for i, (source, target) in enumerate(zip(inputs, (segments_ref, gain_ref, positives_ref), strict=True)):
        small.append(pltpu.make_async_copy(source, target, small_sems.at[i]))
        small[-1].start()
    copies = []
    for at in range(0, tokens, rows):
        copy = pltpu.make_async_copy(hidden_ref.at[0, pl.ds(at, rows)], held.at[pl.ds(at, rows)], sems.at[at // rows])
        copy.start()
        copies.append(copy)
    weights = []
    rank = lax.axis_index("dp")
    small[0].wait()
    segments = segments_ref[...]
    member = jnp.where(lax.broadcasted_iota(jnp.int32, (docs, tokens), 0) == segments, 1.0, 0.0)
    count = jnp.sum(member, axis=1, keepdims=True).astype(jnp.int32)
    document = jnp.transpose(jnp.broadcast_to(segments.astype(F32), (128, tokens)))[:, 0:1].astype(jnp.int32) + rank * docs
    lane = lax.broadcasted_iota(jnp.int32, onehot_ref.shape, 1)
    onehot_ref[...] = jnp.where(lax.rem(lane, n) == document, 1.0, 0.0).astype(BF16)
    lane = lax.broadcasted_iota(jnp.int32, (rows, 128), 1)
    for step, copy in enumerate(copies):
        at = step * rows
        copy.wait()
        states = held[at : at + rows, :].astype(F32)
        mean = jnp.sum(states * states, axis=1, keepdims=True) / width
        scale = lax.rsqrt(mean + EPS)
        side_ref[at : at + rows, :] = jnp.where(lane == 0, scale, scale * scale / width)
        scale_t = jnp.transpose(jnp.broadcast_to(scale, (rows, 128)))[:docs, :]
        weight = member[:, at : at + rows] * scale_t
        weights.append(jnp.concatenate(_high_low(weight), axis=0).astype(BF16))
    small[1].wait()
    small[2].wait()
    weight = jnp.concatenate(weights, axis=1)
    lanes = _pieces(width, POOL_LANES)
    for at in range(0, width, lanes):
        part = jnp.dot(weight, held[:, at : at + lanes], preferred_element_type=F32)
        part_ref[:, at : at + lanes] = (part[:docs, :] + part[docs:, :]) * gain_ref[:, at : at + lanes]
    row = lax.broadcasted_iota(jnp.int32, (docs, EXTRA), 0)
    lane = lax.broadcasted_iota(jnp.int32, (docs, EXTRA), 1)
    own = positives_ref.shape[0]
    first = lax.axis_index("ctx") * own
    positive = jnp.zeros((docs, EXTRA), jnp.int32)
    for i in range(own):
        positive = jnp.where(row == first + i, positives_ref[i], positive)
    digits = jnp.where(lane == 0, count // BASE, 0)
    digits = jnp.where(lane == 1, count % BASE, digits)
    digits = jnp.where(lane == 2, positive // BASE, digits)
    digits = jnp.where(lane == 3, positive % BASE, digits)
    part_ref[:, width:] = digits.astype(F32)


def loss_kernel(n_blocks, *refs):
    blocks = refs[:n_blocks]
    temp_ref, gain_ref, onehot_ref, side_ref, held, grad_hidden_hbm, grad_gain_hbm, loss_hbm = refs[n_blocks : n_blocks + 8]
    emb, scaled, out, grad_gain, loss, sems = refs[n_blocks + 8 :]
    tokens, width = out.shape
    n = emb.shape[0]
    lanes = _pieces(width, LANES)
    group = blocks[0].shape[0]
    own, others = lax.div(lax.axis_index("dp"), 2), n // group
    emb[pl.ds(pl.multiple_of(own * group, group), group), :] = blocks[0][...]
    for k in range(1, others):
        at = (others - 1 - k) * group
        emb[pl.ds(pl.multiple_of((own ^ k) * group, group), group), :] = blocks[1][at : at + group, :]
    gram = lax.dot_general(emb[:, :width], emb[:, :width], (((1,), (1,)), ((), ())), preferred_element_type=F32)
    digits = emb[:, width:].astype(F32)
    digits_t = jnp.transpose(digits)
    count_c = digits[:, 0:1] * BASE + digits[:, 1:2]
    count_r = digits_t[0:1, :] * BASE + digits_t[1:2, :]
    positive_c = (digits[:, 2:3] * BASE + digits[:, 3:4]).astype(jnp.int32)
    positive_r = (digits_t[2:3, :] * BASE + digits_t[3:4, :]).astype(jnp.int32)
    row = lax.broadcasted_iota(jnp.int32, (n, n), 0)
    column = lax.broadcasted_iota(jnp.int32, (n, n), 1)
    same = row == column

    products = jnp.zeros((tokens, n), F32)
    for at in range(0, width, lanes):
        high, low = _high_low(emb[:, at : at + lanes].astype(F32) * gain_ref[:, at : at + lanes])
        high, low = high.astype(BF16), low.astype(BF16)
        scaled[:n, at : at + lanes] = high
        scaled[n : 2 * n, at : at + lanes] = low
        scaled[2 * n :, at : at + lanes] = high
        products += lax.dot_general(held[:, at : at + lanes], high, (((1,), (1,)), ((), ())), preferred_element_type=F32)

    squares = jnp.where(same, gram, 0.0)
    norm_c = lax.rsqrt(jnp.sum(squares, axis=1, keepdims=True) + EPS * count_c * count_c)
    norm_r = lax.rsqrt(jnp.sum(squares, axis=0, keepdims=True) + EPS * count_r * count_r)
    cosine = gram * norm_c * norm_r
    inv_temp = temp_ref[0]
    logits = jnp.where(same, -1e30, cosine * inv_temp)

    def softmax(axis):
        top = jnp.max(logits, axis=axis, keepdims=True)
        expo = jnp.exp(logits - top)
        total = jnp.sum(expo, axis=axis, keepdims=True)
        return top, expo, total

    top, expo, total = softmax(1)
    _, expo_r, total_r = softmax(0)
    pos_c = jnp.where(column == positive_c, 1.0, 0.0)
    pos_r = jnp.where(row == positive_r, 1.0, 0.0)
    terms = top + jnp.log(total) - jnp.sum(pos_c * logits, axis=1, keepdims=True)
    loss[...] = jnp.sum(terms, axis=0, keepdims=True) / n
    loss_copy = pltpu.make_async_copy(loss, loss_hbm, sems.at[0])
    loss_copy.start()
    gmat = ((expo / total - pos_c) * (inv_temp / n)).astype(BF16).astype(F32)
    gmat_t = ((expo_r / total_r - pos_r) * (inv_temp / n)).astype(BF16).astype(F32)
    both = gmat + gmat_t
    along = jnp.sum(both * cosine, axis=1, keepdims=True)
    mix_high, mix_low = _high_low(norm_c * norm_r * (both - jnp.where(same, along, 0.0)))
    mix = jnp.concatenate([mix_high, mix_low], axis=0).astype(BF16)

    wide = jnp.dot(onehot_ref[...], jnp.concatenate([mix] * 3, axis=1), preferred_element_type=F32) * side_ref[:, 0:1]
    pull = jnp.sum(wide[:, :n] * products, axis=1, keepdims=True) * side_ref[:, 1:2]
    high, low = _high_low(wide)
    wide = jnp.where(lax.broadcasted_iota(jnp.int32, wide.shape, 1) < 2 * n, high, low).astype(BF16)
    copies = [loss_copy]
    chunk = _pieces(width, OUT_LANES)
    for left in range(0, width, chunk):
        for at in range(left, left + chunk, lanes):
            spread = jnp.dot(wide, scaled[:, at : at + lanes], preferred_element_type=F32)
            out[:, at : at + lanes] = (spread - held[:, at : at + lanes].astype(F32) * pull).astype(BF16)
            sums = emb[:, at : at + lanes]
            grads = jnp.dot(mix, sums, preferred_element_type=F32)
            grads = jnp.sum((grads[:n, :] + grads[n:, :]) * sums.astype(F32), axis=0, keepdims=True)
            grad_gain[:, at : at + lanes] = grads / gain_ref[:, at : at + lanes]
        copy = pltpu.make_async_copy(
            out.at[:, pl.ds(left, chunk)], grad_hidden_hbm.at[0, :, pl.ds(left, chunk)], sems.at[2 + left // chunk]
        )
        copy.start()
        copies.append(copy)
    copies.append(pltpu.make_async_copy(grad_gain, grad_gain_hbm, sems.at[1]))
    copies[-1].start()
    for copy in copies:
        copy.wait()


def _vmem():
    return pl.BlockSpec(memory_space=pltpu.VMEM)


def _hbm():
    return pl.BlockSpec(memory_space=pltpu.HBM)


def tree_sum(values):
    while len(values) > 1:
        values = [values[i] + values[i + 1] for i in range(0, len(values), 2)]
    return values[0]


def body(dp, ctx, hidden, segments, gain, inv_temp, positives):
    _, tokens, width = hidden.shape
    docs = positives.shape[0] * ctx
    n = docs * dp
    rows = _pieces(tokens, POOL_ROWS)
    d, c = lax.axis_index("dp"), lax.axis_index("ctx")
    core = lax.rem(c, 2)
    gain = gain.reshape(1, width)

    def move(x, to):
        return lax.ppermute(x, BOTH, [(i * ctx + j, to(i, j)[0] * ctx + to(i, j)[1]) for i in range(dp) for j in range(ctx)])

    part, onehot, side, held = pl.pallas_call(
        functools.partial(pool_kernel, docs, n),
        out_shape=(
            jax.ShapeDtypeStruct((docs, width + EXTRA), F32),
            jax.ShapeDtypeStruct((tokens, 2 * n), BF16),
            jax.ShapeDtypeStruct((tokens, 128), F32),
            jax.ShapeDtypeStruct((tokens, width), BF16),
        ),
        in_specs=[_hbm()] * 4,
        out_specs=[_vmem()] * 4,
        scratch_shapes=[
            pltpu.VMEM((1, tokens), jnp.int32),
            pltpu.VMEM((1, width), F32),
            pltpu.SMEM(positives.shape, jnp.int32),
            pltpu.SemaphoreType.DMA((tokens // rows,)),
            pltpu.SemaphoreType.DMA((3,)),
        ],
        compiler_params=pltpu.CompilerParams(vmem_limit_bytes=VMEM_LIMIT),
        name="pool",
    )(*(pltpu.with_memory_space_constraint(x, pltpu.HBM) for x in (hidden, segments, gain, positives)))

    def swap(x):
        return move(x, lambda i, j: (i, j ^ 1))

    chip = (part + swap(part)).astype(BF16)
    lines = ctx // 2
    found = []
    for k in range(lines):
        own = k + 1 if k + 1 < lines else 1
        found.append(move(chip, lambda i, j: (i ^ 1, j ^ (2 * k)) if j % 2 else (i, j ^ (2 * own))))
    terms = [jnp.where(core == 0, left, right) for left, right in zip([chip] + found[:-1], found, strict=True)]
    block = tree_sum([x.astype(F32) for x in terms]).astype(BF16)

    groups = dp // 2
    even = lax.rem(core + d, 2) == 0

    def both(mine, theirs):
        pairs = jnp.stack([jnp.where(even, mine, theirs), jnp.where(even, theirs, mine)], axis=1)
        return pairs.reshape(-1, width + EXTRA)

    far = [move(block, lambda i, j: (i ^ (2 * k), j)) for k in range(groups - 1, 0, -1)]
    blocks = [both(block[None], swap(block)[None])]
    if far:
        far = jnp.stack(far)
        blocks.append(both(far, swap(far)))

    grad_hidden, grad_gain, loss = pl.pallas_call(
        functools.partial(loss_kernel, len(blocks)),
        out_shape=(
            jax.ShapeDtypeStruct((1, tokens, width), BF16),
            jax.ShapeDtypeStruct((1, width), F32),
            jax.ShapeDtypeStruct((1, 1), F32),
        ),
        in_specs=[_vmem()] * len(blocks) + [pl.BlockSpec(memory_space=pltpu.SMEM)] + [_vmem()] * 4,
        out_specs=(_hbm(), _hbm(), _hbm()),
        scratch_shapes=[
            pltpu.VMEM((n, width + EXTRA), BF16),
            pltpu.VMEM((3 * n, width), BF16),
            pltpu.VMEM((tokens, width), BF16),
            pltpu.VMEM((1, width), F32),
            pltpu.VMEM((1, 1), F32),
            pltpu.SemaphoreType.DMA((2 + width // _pieces(width, OUT_LANES),)),
        ],
        compiler_params=pltpu.CompilerParams(vmem_limit_bytes=VMEM_LIMIT),
        name="loss",
    )(*blocks, inv_temp.reshape(1), gain, onehot, side, held)
    return grad_hidden, grad_gain.reshape(width), loss.reshape(())


def solution(mesh):
    return jax.shard_map(
        functools.partial(body, mesh.shape["dp"], mesh.shape["ctx"]),
        mesh=mesh,
        in_specs=(P("dp", "ctx", None), P("dp", "ctx"), P(), P(), P(("dp", "ctx"))),
        out_specs=(P("dp", "ctx", None), P(), P()),
        check_vma=False,
    )
```

```python
import functools

import jax
import jax.numpy as jnp
from jax import lax
from jax.experimental import pallas as pl
from jax.experimental.pallas import tpu as pltpu
from jax.sharding import PartitionSpec as P

EPS = 1e-06
EXTRA = 128
BASE = 16
POOL_ROWS = 128
POOL_LANES = 1024
OUT_LANES = 512
LANES = 256
BOTH = ("dp", "ctx")
VMEM_LIMIT = 32 * 1024 * 1024
F32, BF16 = jnp.float32, jnp.bfloat16


def _pieces(size, want):
    return want if size % want == 0 else size


def _high_low(x):
    high = x.astype(BF16).astype(F32)
    return high, x - high


def pool_kernel(docs, n, *refs):
    hidden_ref, *inputs, part_ref, onehot_ref, side_ref, held = refs[:8]
    segments_ref, gain_ref, positives_ref, sems, small_sems = refs[8:]
    tokens, width = held.shape
    rows = _pieces(tokens, POOL_ROWS)
    small = []
    for i, (source, target) in enumerate(zip(inputs, (segments_ref, gain_ref, positives_ref), strict=True)):
        small.append(pltpu.make_async_copy(source, target, small_sems.at[i]))
        small[-1].start()
    copies = []
    for at in range(0, tokens, rows):
        copy = pltpu.make_async_copy(hidden_ref.at[0, pl.ds(at, rows)], held.at[pl.ds(at, rows)], sems.at[at // rows])
        copy.start()
        copies.append(copy)
    weights = []
    rank = lax.axis_index("dp")
    small[0].wait()
    segments = segments_ref[...]
    member = jnp.where(lax.broadcasted_iota(jnp.int32, (docs, tokens), 0) == segments, 1.0, 0.0)
    count = jnp.sum(member, axis=1, keepdims=True).astype(jnp.int32)
    document = jnp.transpose(jnp.broadcast_to(segments.astype(F32), (128, tokens)))[:, 0:1].astype(jnp.int32) + rank * docs
    lane = lax.broadcasted_iota(jnp.int32, onehot_ref.shape, 1)
    onehot_ref[...] = jnp.where(lax.rem(lane, n) == document, 1.0, 0.0).astype(BF16)
    lane = lax.broadcasted_iota(jnp.int32, (rows, 128), 1)
    for step, copy in enumerate(copies):
        at = step * rows
        copy.wait()
        states = held[at : at + rows, :].astype(F32)
        mean = jnp.sum(states * states, axis=1, keepdims=True) / width
        scale = lax.rsqrt(mean + EPS)
        side_ref[at : at + rows, :] = jnp.where(lane == 0, scale, scale * scale / width)
        scale_t = jnp.transpose(jnp.broadcast_to(scale, (rows, 128)))[:docs, :]
        weight = member[:, at : at + rows] * scale_t
        weights.append(jnp.concatenate(_high_low(weight), axis=0).astype(BF16))
    small[1].wait()
    small[2].wait()
    weight = jnp.concatenate(weights, axis=1)
    lanes = _pieces(width, POOL_LANES)
    for at in range(0, width, lanes):
        part = jnp.dot(weight, held[:, at : at + lanes], preferred_element_type=F32)
        part_ref[:, at : at + lanes] = (part[:docs, :] + part[docs:, :]) * gain_ref[:, at : at + lanes]
    row = lax.broadcasted_iota(jnp.int32, (docs, EXTRA), 0)
    lane = lax.broadcasted_iota(jnp.int32, (docs, EXTRA), 1)
    own = positives_ref.shape[0]
    first = lax.axis_index("ctx") * own
    positive = jnp.zeros((docs, EXTRA), jnp.int32)
    for i in range(own):
        positive = jnp.where(row == first + i, positives_ref[i], positive)
    digits = jnp.where(lane == 0, count // BASE, 0)
    digits = jnp.where(lane == 1, count % BASE, digits)
    digits = jnp.where(lane == 2, positive // BASE, digits)
    digits = jnp.where(lane == 3, positive % BASE, digits)
    part_ref[:, width:] = digits.astype(F32)


def loss_kernel(n_blocks, *refs):
    blocks = refs[:n_blocks]
    temp_ref, gain_ref, onehot_ref, side_ref, held, grad_hidden_hbm, grad_gain_hbm, loss_hbm = refs[n_blocks : n_blocks + 8]
    emb, scaled, out, grad_gain, loss, sems = refs[n_blocks + 8 :]
    tokens, width = out.shape
    n = emb.shape[0]
    lanes = _pieces(width, LANES)
    group = blocks[0].shape[0]
    own, others = lax.div(lax.axis_index("dp"), 2), n // group
    emb[pl.ds(pl.multiple_of(own * group, group), group), :] = blocks[0][...]
    for k in range(1, others):
        at = (others - 1 - k) * group
        emb[pl.ds(pl.multiple_of((own ^ k) * group, group), group), :] = blocks[1][at : at + group, :]
    gram = lax.dot_general(emb[:, :width], emb[:, :width], (((1,), (1,)), ((), ())), preferred_element_type=F32)
    digits = emb[:, width:].astype(F32)
    digits_t = jnp.transpose(digits)
    count_c = digits[:, 0:1] * BASE + digits[:, 1:2]
    count_r = digits_t[0:1, :] * BASE + digits_t[1:2, :]
    positive_c = (digits[:, 2:3] * BASE + digits[:, 3:4]).astype(jnp.int32)
    positive_r = (digits_t[2:3, :] * BASE + digits_t[3:4, :]).astype(jnp.int32)
    row = lax.broadcasted_iota(jnp.int32, (n, n), 0)
    column = lax.broadcasted_iota(jnp.int32, (n, n), 1)
    same = row == column

    products = jnp.zeros((tokens, n), F32)
    for at in range(0, width, lanes):
        high, low = _high_low(emb[:, at : at + lanes].astype(F32) * gain_ref[:, at : at + lanes])
        high, low = high.astype(BF16), low.astype(BF16)
        scaled[:n, at : at + lanes] = high
        scaled[n : 2 * n, at : at + lanes] = low
        scaled[2 * n :, at : at + lanes] = high
        products += lax.dot_general(held[:, at : at + lanes], high, (((1,), (1,)), ((), ())), preferred_element_type=F32)

    squares = jnp.where(same, gram, 0.0)
    norm_c = lax.rsqrt(jnp.sum(squares, axis=1, keepdims=True) + EPS * count_c * count_c)
    norm_r = lax.rsqrt(jnp.sum(squares, axis=0, keepdims=True) + EPS * count_r * count_r)
    cosine = gram * norm_c * norm_r
    inv_temp = temp_ref[0]
    logits = jnp.where(same, -1e30, cosine * inv_temp)

    def softmax(axis):
        top = jnp.max(logits, axis=axis, keepdims=True)
        expo = jnp.exp(logits - top)
        total = jnp.sum(expo, axis=axis, keepdims=True)
        return top, expo, total

    top, expo, total = softmax(1)
    _, expo_r, total_r = softmax(0)
    pos_c = jnp.where(column == positive_c, 1.0, 0.0)
    pos_r = jnp.where(row == positive_r, 1.0, 0.0)
    terms = top + jnp.log(total) - jnp.sum(pos_c * logits, axis=1, keepdims=True)
    loss[...] = jnp.sum(terms, axis=0, keepdims=True) / n
    loss_copy = pltpu.make_async_copy(loss, loss_hbm, sems.at[0])
    loss_copy.start()
    gmat = ((expo / total - pos_c) * (inv_temp / n)).astype(BF16).astype(F32)
    gmat_t = ((expo_r / total_r - pos_r) * (inv_temp / n)).astype(BF16).astype(F32)
    both = gmat + gmat_t
    along = jnp.sum(both * cosine, axis=1, keepdims=True)
    mix_high, mix_low = _high_low(norm_c * norm_r * (both - jnp.where(same, along, 0.0)))
    mix = jnp.concatenate([mix_high, mix_low], axis=0).astype(BF16)

    wide = jnp.dot(onehot_ref[...], jnp.concatenate([mix] * 3, axis=1), preferred_element_type=F32) * side_ref[:, 0:1]
    pull = jnp.sum(wide[:, :n] * products, axis=1, keepdims=True) * side_ref[:, 1:2]
    high, low = _high_low(wide)
    wide = jnp.where(lax.broadcasted_iota(jnp.int32, wide.shape, 1) < 2 * n, high, low).astype(BF16)
    copies = [loss_copy]
    chunk = _pieces(width, OUT_LANES)
    for left in range(0, width, chunk):
        for at in range(left, left + chunk, lanes):
            spread = jnp.dot(wide, scaled[:, at : at + lanes], preferred_element_type=F32)
            out[:, at : at + lanes] = (spread - held[:, at : at + lanes].astype(F32) * pull).astype(BF16)
        copy = pltpu.make_async_copy(
            out.at[:, pl.ds(left, chunk)], grad_hidden_hbm.at[0, :, pl.ds(left, chunk)], sems.at[2 + left // chunk]
        )
        copy.start()
        copies.append(copy)
    for at in range(0, width, lanes):
        sums = emb[:, at : at + lanes]
        grads = jnp.dot(mix, sums, preferred_element_type=F32)
        grads = jnp.sum((grads[:n, :] + grads[n:, :]) * sums.astype(F32), axis=0, keepdims=True)
        grad_gain[:, at : at + lanes] = grads / gain_ref[:, at : at + lanes]
    copies.append(pltpu.make_async_copy(grad_gain, grad_gain_hbm, sems.at[1]))
    copies[-1].start()
    for copy in copies:
        copy.wait()


def _vmem():
    return pl.BlockSpec(memory_space=pltpu.VMEM)


def _hbm():
    return pl.BlockSpec(memory_space=pltpu.HBM)


def tree_sum(values):
    while len(values) > 1:
        values = [values[i] + values[i + 1] for i in range(0, len(values), 2)]
    return values[0]


def body(dp, ctx, hidden, segments, gain, inv_temp, positives):
    _, tokens, width = hidden.shape
    docs = positives.shape[0] * ctx
    n = docs * dp
    rows = _pieces(tokens, POOL_ROWS)
    d, c = lax.axis_index("dp"), lax.axis_index("ctx")
    core = lax.rem(c, 2)
    gain = gain.reshape(1, width)

    def move(x, to):
        return lax.ppermute(x, BOTH, [(i * ctx + j, to(i, j)[0] * ctx + to(i, j)[1]) for i in range(dp) for j in range(ctx)])

    part, onehot, side, held = pl.pallas_call(
        functools.partial(pool_kernel, docs, n),
        out_shape=(
            jax.ShapeDtypeStruct((docs, width + EXTRA), F32),
            jax.ShapeDtypeStruct((tokens, 2 * n), BF16),
            jax.ShapeDtypeStruct((tokens, 128), F32),
            jax.ShapeDtypeStruct((tokens, width), BF16),
        ),
        in_specs=[_hbm()] * 4,
        out_specs=[_vmem()] * 4,
        scratch_shapes=[
            pltpu.VMEM((1, tokens), jnp.int32),
            pltpu.VMEM((1, width), F32),
            pltpu.SMEM(positives.shape, jnp.int32),
            pltpu.SemaphoreType.DMA((tokens // rows,)),
            pltpu.SemaphoreType.DMA((3,)),
        ],
        compiler_params=pltpu.CompilerParams(vmem_limit_bytes=VMEM_LIMIT),
        name="pool",
    )(*(pltpu.with_memory_space_constraint(x, pltpu.HBM) for x in (hidden, segments, gain, positives)))

    def swap(x):
        return move(x, lambda i, j: (i, j ^ 1))

    chip = (part + swap(part)).astype(BF16)
    lines = ctx // 2
    found = []
    for k in range(lines):
        own = k + 1 if k + 1 < lines else 1
        found.append(move(chip, lambda i, j: (i ^ 1, j ^ (2 * k)) if j % 2 else (i, j ^ (2 * own))))
    terms = [jnp.where(core == 0, left, right) for left, right in zip([chip] + found[:-1], found, strict=True)]
    block = tree_sum([x.astype(F32) for x in terms]).astype(BF16)

    groups = dp // 2
    even = lax.rem(core + d, 2) == 0

    def both(mine, theirs):
        pairs = jnp.stack([jnp.where(even, mine, theirs), jnp.where(even, theirs, mine)], axis=1)
        return pairs.reshape(-1, width + EXTRA)

    far = [move(block, lambda i, j: (i ^ (2 * k), j)) for k in range(groups - 1, 0, -1)]
    blocks = [both(block[None], swap(block)[None])]
    if far:
        far = jnp.stack(far)
        blocks.append(both(far, swap(far)))

    grad_hidden, grad_gain, loss = pl.pallas_call(
        functools.partial(loss_kernel, len(blocks)),
        out_shape=(
            jax.ShapeDtypeStruct((1, tokens, width), BF16),
            jax.ShapeDtypeStruct((1, width), F32),
            jax.ShapeDtypeStruct((1, 1), F32),
        ),
        in_specs=[_vmem()] * len(blocks) + [pl.BlockSpec(memory_space=pltpu.SMEM)] + [_vmem()] * 4,
        out_specs=(_hbm(), _hbm(), _hbm()),
        scratch_shapes=[
            pltpu.VMEM((n, width + EXTRA), BF16),
            pltpu.VMEM((3 * n, width), BF16),
            pltpu.VMEM((tokens, width), BF16),
            pltpu.VMEM((1, width), F32),
            pltpu.VMEM((1, 1), F32),
            pltpu.SemaphoreType.DMA((2 + width // _pieces(width, OUT_LANES),)),
        ],
        compiler_params=pltpu.CompilerParams(vmem_limit_bytes=VMEM_LIMIT),
        name="loss",
    )(*blocks, inv_temp.reshape(1), gain, onehot, side, held)
    return grad_hidden, grad_gain.reshape(width), loss.reshape(())


def solution(mesh):
    return jax.shard_map(
        functools.partial(body, mesh.shape["dp"], mesh.shape["ctx"]),
        mesh=mesh,
        in_specs=(P("dp", "ctx", None), P("dp", "ctx"), P(), P(), P(("dp", "ctx"))),
        out_specs=(P("dp", "ctx", None), P(), P()),
        check_vma=False,
    )
```
